128 devices in a mesh: expert: 4 (over y), feat: 32 (over x, z, core).
Axes of the slice: x: 4, y: 4, z: 4, core: 2. Of those that a mesh axis runs over, the one named last changes fastest.
Arguments:
- tokens: bfloat16 [1024, 4096], P(('expert', 'feat')), may hold values from -6 to 6
- expert_ids: int32 [1024, 2], P(('expert', 'feat')), may hold values from 0 to 7, as said below
- route_weights: bfloat16 [1024, 2], P(('expert', 'feat')), may hold values from 0.099609375 to 1
- gate_proj: bfloat16 [4096, 28672], P(None, ('expert', 'feat')), may hold values from -0.09375 to 0.09375
- up_proj: bfloat16 [4096, 28672], P(None, ('expert', 'feat')), may hold values from -0.09375 to 0.09375
- down_proj: bfloat16 [28672, 4096], P(('expert', 'feat')), may hold values from -0.046875 to 0.046875
- enc_weight: float32 [4096, 32768], P(None, ('expert', 'feat')), may hold values from -0.09375 to 0.09375
- enc_bias: float32 [32768], P(('expert', 'feat')), may hold values from -3 to 3
- log_threshold: float32 [32768], P(('expert', 'feat')), may hold values from -2.3 to 0
- dec_weight: float32 [32768, 4096], P(('expert', 'feat')), may hold values from -0.046875 to 0.046875
Outputs:
- grad_encoder: float32 [4096, 32768], P(None, ('expert', 'feat'))
- grad_decoder: float32 [32768, 4096], P(('expert', 'feat'))
- grad_bias: float32 [32768], P(('expert', 'feat'))
- grad_threshold: float32 [32768], P(('expert', 'feat'))
The draws below stay inside these ranges and needn't reach their ends.
Inputs may be any that keep to these rules, and one draw needn't show every extreme that they name: `expert_ids`: each token names two different experts of 0 to 7. Among the 8 tokens of one device, each expert below 2 is named by at most 4 tokens; in every draw one of these experts, drawn from the seed and the same for all devices, is named by exactly 4 tokens of every device.
All inputs are finite; a program needn't handle non-finite values.
Results may differ from the reference program's by a relative error of at most 0.0021.
Values may be sent and summed in bfloat16 or wider, within the bound.
A program may use at most 128 MiB of HBM per device.

```python
import math
import jax
import jax.numpy as jnp
from jax import lax

D = 4096
FF = 14336
ROUTED = 8
FEATURES = 16384
TOK_DEV = 8
TOKENS = 1024
EXPERTS = 2


def draw_expert_ids(key, part):
    blocks = TOKENS // TOK_DEV
    capacity = TOK_DEV // 2
    outside = ROUTED - EXPERTS
    keys = jax.random.split(key, 8)
    hottest = jax.random.randint(keys[0], (), 0, EXPERTS)
    scores = jax.random.randint(keys[1], (blocks, TOK_DEV), 0, 1 << 20) * TOK_DEV + jnp.arange(TOK_DEV, dtype=jnp.int32)[None, :]
    order = jnp.argsort(scores, axis=1)
    ranks = jnp.argsort(order, axis=1)
    is_hot = ranks < capacity
    colder = jnp.remainder(hottest + 1 + jax.random.randint(keys[2], (blocks, TOK_DEV), 0, max(EXPERTS - 1, 1)), EXPERTS)
    picked = jax.random.randint(keys[3], (blocks, TOK_DEV), 0, 4) == 0
    far_one = EXPERTS + jax.random.randint(keys[4], (blocks, TOK_DEV), 0, outside)
    first = jnp.where(is_hot, hottest, jnp.where(picked, colder, far_one))
    step_over = jax.random.randint(keys[5], (blocks, TOK_DEV), 0, outside - 1)
    other_far = EXPERTS + jax.random.randint(keys[6], (blocks, TOK_DEV), 0, outside)
    second = jnp.where(first >= EXPERTS, EXPERTS + jnp.remainder(first - EXPERTS + 1 + step_over, outside), other_far)
    swapped = jax.random.randint(keys[7], (blocks, TOK_DEV), 0, 2) == 1
    left = jnp.where(swapped, second, first)
    right = jnp.where(swapped, first, second)
    return jnp.stack([left, right], axis=-1).reshape(TOKENS, 2).astype(jnp.int32)


def block_levels(key, dims, cuts, low, top_value):
    level, own = 1.0, jax.random.fold_in(key, 6)
    for axis_at, blocks in cuts:
        steps = jnp.exp(jax.random.uniform(jax.random.fold_in(own, axis_at), (blocks,), jnp.float32, low / len(cuts), top_value / len(cuts)))
        level = level * jnp.repeat(steps, dims[axis_at] // blocks).reshape([-1 if axis == axis_at else 1 for axis in range(len(dims))])
    return level


def bell_draw(own_key, shape, scale, limit, pieces=(), kind=jnp.bfloat16):
    entries = jax.random.normal(own_key, shape, jnp.float32) * scale
    if len(pieces) > 0:
        entries = block_levels(own_key, shape, pieces, -0.22, 0.18) * entries
    return jnp.clip(entries, min=-limit, max=limit).astype(kind)


def setup_inputs(seed: int = 0) -> dict:
    seeds = jax.random.split(jax.random.key(seed), 11)
    tokens = bell_draw(seeds[0], (TOKENS, D), 1.0, 6.0, ((0, 128),))
    expert_ids = draw_expert_ids(jax.random.fold_in(seeds[10], 71), 0)
    route_weights = jnp.clip(jnp.exp(math.log(1.0) - 2.306499 * jax.random.uniform(seeds[2], (TOKENS, 2), jnp.float32) ** block_levels(seeds[2], (TOKENS, 2), ((0, 128),), -0.2, 0.2)), 0.099609375, 1.0).astype(jnp.bfloat16)
    gate_proj = bell_draw(seeds[3], (D, EXPERTS * FF), D ** -0.5, 0.09375, ((1, 128),))
    up_proj = bell_draw(seeds[4], (D, EXPERTS * FF), D ** -0.5, 0.09375, ((1, 128),))
    down_proj = bell_draw(seeds[5], (EXPERTS * FF, D), FF ** -0.5, 0.046875, ((0, 128),))
    enc_weight = bell_draw(seeds[6], (D, EXPERTS * FEATURES), D ** -0.5, 0.09375, ((1, 128),), jnp.float32)
    enc_bias = bell_draw(seeds[7], (EXPERTS * FEATURES,), 0.5, 3.0, ((0, 128),), jnp.float32)
    log_threshold = jnp.clip(-2.3 + 2.3 * jax.random.uniform(seeds[8], (EXPERTS * FEATURES,), jnp.float32) ** block_levels(seeds[8], (EXPERTS * FEATURES,), ((0, 128),), -0.2, 0.2), -2.3, 0.0)
    dec_weight = bell_draw(seeds[9], (EXPERTS * FEATURES, D), FEATURES ** -0.5, 0.046875, ((0, 128),), jnp.float32)
    return dict(tokens=tokens, expert_ids=expert_ids, route_weights=route_weights, gate_proj=gate_proj, up_proj=up_proj, down_proj=down_proj, enc_weight=enc_weight, enc_bias=enc_bias, log_threshold=log_threshold, dec_weight=dec_weight)


sharpness = 0.1
kernel_width = 0.5
density_weight = 0.01
highest = lax.Precision.HIGHEST


def expert_gradients(tokens, token_weight, gate_part, up_part, down_part, enc_part, bias_part, log_part, dec_part):
    gate_act = jnp.dot(tokens, gate_part, preferred_element_type=jnp.float32)
    up_act = jnp.dot(tokens, up_part, preferred_element_type=jnp.float32)
    hidden = (jax.nn.silu(gate_act) * up_act).astype(jnp.bfloat16)
    target = jnp.dot(hidden, down_part, preferred_element_type=jnp.float32)
    inputs = tokens.astype(jnp.float32)
    preact = jnp.dot(inputs, enc_part, precision=highest) + bias_part
    threshold = jnp.exp(log_part)
    shifted = preact - threshold
    soft_gate = jax.nn.sigmoid(shifted / sharpness)
    active = preact * soft_gate
    recon_error = jnp.dot(active, dec_part, precision=highest) - target
    residual_grad = 2.0 * token_weight[:, None] * recon_error
    grad_decoder = jnp.dot(active.T, residual_grad, precision=highest)
    grad_active = jnp.dot(residual_grad, dec_part.T, precision=highest)
    grad_pre = grad_active * soft_gate
    grad_encoder = jnp.dot(inputs.T, grad_pre, precision=highest)
    grad_bias = jnp.sum(grad_pre, axis=0)
    kernel = jnp.maximum(0.0, 1.0 - jnp.abs(shifted) / kernel_width) / kernel_width
    slope_sum = jnp.sum((grad_active * threshold + density_weight * token_weight[:, None]) * kernel, axis=0)
    return grad_encoder, grad_decoder, grad_bias, -threshold * slope_sum


def reference(tokens, expert_ids, route_weights, gate_proj, up_proj, down_proj, enc_weight, enc_bias, log_threshold, dec_weight):
    enc_list, dec_list, bias_list, thresh_list = [], [], [], []
    weights32 = route_weights.astype(jnp.float32)
    for index in range(EXPERTS):
        token_weight = jnp.sum(jnp.where(expert_ids == index, weights32, 0.0), axis=1)
        hid_lo, hid_hi = index * FF, (index + 1) * FF
        feat_lo, feat_hi = index * FEATURES, (index + 1) * FEATURES
        result = expert_gradients(tokens, token_weight, gate_proj[:, hid_lo:hid_hi], up_proj[:, hid_lo:hid_hi], down_proj[hid_lo:hid_hi, :], enc_weight[:, feat_lo:feat_hi], enc_bias[feat_lo:feat_hi], log_threshold[feat_lo:feat_hi], dec_weight[feat_lo:feat_hi, :])
        enc_list.append(result[0])
        dec_list.append(result[1])
        bias_list.append(result[2])
        thresh_list.append(result[3])
    return (jnp.concatenate(enc_list, axis=1), jnp.concatenate(dec_list, axis=0), jnp.concatenate(bias_list, axis=0), jnp.concatenate(thresh_list, axis=0))
```

```python
import jax
import jax.numpy as jnp
from jax import lax
from jax.sharding import PartitionSpec as P

sharpness = 0.1
kernel_width = 0.5
density_weight = 0.01


def partner(block, axis, stride):
    count = lax.axis_size(axis)
    route = []
    for low in range(count):
        high = low | 1 << stride
        if high != low and high < count:
            route += [(low, high), (high, low)]
    return lax.ppermute(block, axis, route)


def pack_slots(tokens, expert_ids, route_weights, experts):
    capacity = tokens.shape[0] // 2
    window = jnp.arange(experts, dtype=jnp.int32)
    matches = expert_ids[:, :, None] == window[None, None, :]
    named = jnp.sum(matches.astype(jnp.int32), axis=1)
    weighted = jnp.sum(
        jnp.where(matches, route_weights[:, :, None], jnp.zeros((), jnp.bfloat16)), axis=1
    )
    rows = jnp.arange(tokens.shape[0], dtype=jnp.int32)
    earlier = rows[None, :, None] < rows[:, None, None]
    slot_index = jnp.sum(jnp.where(earlier, named[None, :, :], 0), axis=1)
    places = jnp.arange(capacity, dtype=jnp.int32)
    chosen = (named.T[:, None, :] == 1) & (slot_index.T[:, None, :] == places[None, :, None])
    slot_rows = jnp.einsum(
        "ect,td->ecd", chosen.astype(jnp.bfloat16), tokens, preferred_element_type=jnp.float32
    ).astype(jnp.bfloat16)
    slot_weights = jnp.sum(
        jnp.where(chosen, weighted.T[:, None, :], jnp.zeros((), jnp.bfloat16)), axis=2
    )
    return (slot_rows, slot_weights)


def split(value):
    high = lax.reduce_precision(value, 8, 7)
    return high.astype(jnp.bfloat16), (value - high).astype(jnp.bfloat16)


def product(left, right, dims):
    return lax.dot_general(left, right, (dims, ((), ())), preferred_element_type=jnp.float32)


def body(
    tokens,
    expert_ids,
    route_weights,
    gate_proj,
    up_proj,
    down_proj,
    enc_weight,
    enc_bias,
    log_threshold,
    dec_weight,
):
    copies = 2
    experts = lax.axis_size("expert") // copies
    slot_rows, slot_weights = pack_slots(tokens, expert_ids, route_weights, experts)
    send_rows = jnp.repeat(slot_rows, copies, axis=0)
    send_weights = jnp.repeat(slot_weights, copies, axis=0)
    came_rows, came_weights = (
        lax.all_to_all(send_rows, "expert", split_axis=0, concat_axis=0, tiled=True),
        lax.all_to_all(send_weights, "expert", split_axis=0, concat_axis=0, tiled=True),
    )
    all_rows, all_weights = (
        lax.all_gather(came_rows, "feat", axis=0, tiled=True),
        lax.all_gather(came_weights, "feat", axis=0, tiled=True),
    )
    width = tokens.shape[1]
    token_rows = all_rows.reshape(-1, width)
    row_weights = all_weights.reshape(-1).astype(jnp.float32)
    gate_act = jnp.dot(token_rows, gate_proj, preferred_element_type=jnp.float32)
    up_act = jnp.dot(token_rows, up_proj, preferred_element_type=jnp.float32)
    hidden = (jax.nn.silu(gate_act) * up_act).astype(jnp.bfloat16)
    target_part = jnp.dot(hidden, down_proj, preferred_element_type=jnp.float32)
    rows = ((1,), (0,))
    down = ((0,), (0,))
    enc_high, enc_low = split(enc_weight)
    dec_high, dec_low = split(dec_weight)
    preact = product(token_rows, enc_high, rows) + product(token_rows, enc_low, rows) + enc_bias
    threshold = jnp.exp(log_threshold)
    shifted = preact - threshold
    soft_gate = jax.nn.sigmoid(shifted / sharpness)
    active = preact * soft_gate
    act_high, act_low = split(active)
    recon = product(act_high, dec_high, rows) + product(act_high, dec_low, rows)
    partial_error = recon + product(act_low, dec_high, rows) - target_part
    feat_total = lax.psum_scatter(partial_error, "feat", scatter_dimension=0, tiled=True)
    recon_error = feat_total + partner(feat_total, "expert", 0)
    own_rows = feat_total.shape[0]
    own_weights = lax.dynamic_slice_in_dim(row_weights, lax.axis_index("feat") * own_rows, own_rows)
    own_grad = (2.0 * own_weights[:, None] * recon_error).astype(jnp.bfloat16)
    residual_grad = lax.all_gather(own_grad, "feat", axis=0, tiled=True)
    grad_decoder = product(act_high, residual_grad, down) + product(act_low, residual_grad, down)
    across = ((1,), (1,))
    grad_active = product(residual_grad, dec_high, across) + product(residual_grad, dec_low, across)
    grad_pre = grad_active * soft_gate
    pre_high, pre_low = split(grad_pre)
    grad_encoder = product(token_rows, pre_high, down) + product(token_rows, pre_low, down)
    grad_bias = jnp.sum(grad_pre, axis=0)
    kernel = jnp.maximum(0.0, 1.0 - jnp.abs(shifted) / kernel_width) / kernel_width
    slope_sum = jnp.sum(
        (grad_active * threshold + density_weight * row_weights[:, None]) * kernel, axis=0
    )
    grad_threshold = -threshold * slope_sum
    return (grad_encoder, grad_decoder, grad_bias, grad_threshold)


def solution(mesh):
    in_specs = (
        P(("expert", "feat"), None),
        P(("expert", "feat"), None),
        P(("expert", "feat"), None),
        P(None, ("expert", "feat")),
        P(None, ("expert", "feat")),
        P(("expert", "feat"), None),
        P(None, ("expert", "feat")),
        P(("expert", "feat")),
        P(("expert", "feat")),
        P(("expert", "feat"), None),
    )
    out_specs = (
        P(None, ("expert", "feat")),
        P(("expert", "feat"), None),
        P(("expert", "feat")),
        P(("expert", "feat")),
    )
    return jax.shard_map(body, mesh=mesh, in_specs=in_specs, out_specs=out_specs, check_vma=False)
```

```python
import functools

import jax
import jax.numpy as jnp
from jax import lax
from jax.experimental import pallas as pl
from jax.experimental.pallas import tpu as pltpu
from jax.sharding import PartitionSpec as P

MESH = pl.DeviceIdType.MESH
f32 = jnp.float32
bf16 = jnp.bfloat16

sharpness = 0.1
kernel_width = 0.5
density_weight = 0.01

CHUNKS = 2
LANES = 128
UNIT = 16
BLOCK = 4 * UNIT
HALF = 4 * BLOCK
ROWS = 2 * HALF


def dot(left, right):
    return jnp.dot(left, right, preferred_element_type=f32)


def dot_nt(left, right):
    return lax.dot_general(left, right, (((1,), (1,)), ((), ())), preferred_element_type=f32)


def dot_tn(left, right):
    return lax.dot_general(left, right, (((0,), (0,)), ((), ())), preferred_element_type=f32)


def split(value):
    high = value.astype(bf16)
    return high, (value - high.astype(f32)).astype(bf16)


def encode(value, out, rows):
    width = value.shape[1]
    largest = jnp.max(jnp.abs(value), axis=1, keepdims=True)
    power = jnp.ceil(jnp.log2(jnp.maximum(largest, 1e-30)))
    out[rows, 0:width] = jnp.round(value * jnp.exp2(14.0 - power)).astype(jnp.int32).astype(jnp.int16)
    lanes = jnp.broadcast_to(power.astype(jnp.int32), (value.shape[0], LANES))
    out[rows, width : width + LANES] = lanes.astype(jnp.int16)


def decode(ref, rows):
    width = ref.shape[1] - LANES
    power = ref[rows, width : width + LANES].astype(jnp.int32).astype(f32)[:, 0:1]
    return ref[rows, 0:width].astype(jnp.int32).astype(f32) * jnp.exp2(power - 14.0)


def each(count, step):
    lax.fori_loop(0, count, lambda i, carry: (step(i), carry)[1], 0)


def al(start, size):
    return pl.ds(pl.multiple_of(start, 16), size)


def forward_kernel(
    tokens,
    ids,
    weights,
    bias,
    log_threshold,
    gate_hbm,
    up_hbm,
    down_hbm,
    enc_hbm,
    dec_hbm,
    rows_out,
    grad_out,
    act_high_out,
    act_low_out,
    pre_high_out,
    pre_low_out,
    bias_out,
    threshold_out,
    enc_stage,
    dec_stage,
    gate_w,
    up_w,
    enc_w,
    dec_w,
    pack32,
    pack,
    ybuf,
    unit32,
    trows,
    rgrad,
    acc_gate,
    acc_up,
    acc_pre,
    left,
    gate_s,
    shift_s,
    acc_grad,
    psib,
    pown,
    sib_out,
    sib_in,
    b1_out,
    b1_in,
    b2_out,
    b2_in,
    a_out,
    a_in,
    y_out,
    y_in,
    send_sem,
    recv_sem,
    ysend_sem,
    yrecv_sem,
    local_sem,
):
    width = tokens.shape[1]
    cols = width // CHUNKS
    hidden_width = gate_w.shape[1]
    features = enc_w.shape[1] // 2
    piece = width // 4

    y = lax.axis_index("expert")
    feat = lax.axis_index("feat")
    core = lax.rem(feat, 2)
    z = lax.rem(feat // 2, 4)
    x = feat // 8
    a = x + core * (z - x)
    b = z + core * (x - z)

    def a_peer(k):
        ax = lax.rem(x + (1 - core) * k, 4)
        az = lax.rem(z + core * k, 4)
        return (y, (ax * 4 + az) * 2 + core)

    def b_peer(k):
        bx = lax.rem(x + core * k, 4)
        bz = lax.rem(z + (1 - core) * k, 4)
        return (y, (bx * 4 + bz) * 2 + core)

    def y_peer(k):
        return (lax.rem(y + k, 4), feat)

    sibling = (y, feat + 1 - 2 * core)
    partner = (y + 1 - 2 * lax.rem(y, 2), feat)

    loads = [
        pltpu.make_async_copy(src, dst, local_sem.at[i])
        for i, (src, dst) in enumerate(
            [
                (enc_hbm, enc_stage),
                (dec_hbm, dec_stage),
                (gate_hbm, gate_w),
                (up_hbm, up_w),
                (down_hbm, dec_w.at[pl.ds(3 * features, hidden_width)]),
            ]
        )
    ]
    for load in loads:
        load.start()

    barrier = pltpu.get_barrier_semaphore()
    peers = [a_peer(k) for k in (1, 2, 3)] + [b_peer(k) for k in (1, 3)] + [y_peer(k) for k in (1, 2, 3)] + [sibling]
    for peer in peers:
        pl.semaphore_signal(barrier, inc=1, device_id=peer, device_id_type=MESH)

    row_id = lax.broadcasted_iota(jnp.int32, (8, 1), 0)
    values = tokens[...].astype(f32)
    route = weights[...].astype(f32)
    for expert in range(2):
        match = ids[...] == expert
        named = jnp.sum(jnp.where(match, 1.0, 0.0), axis=1, keepdims=True)
        weight = jnp.sum(jnp.where(match, route, 0.0), axis=1, keepdims=True)
        slot = jnp.zeros((8, 1), f32)
        for t in range(7):
            slot += jnp.where(row_id > t, named[t : t + 1, :], 0.0)
        pack32[...] = jnp.zeros_like(pack32)
        for c in range(4):
            chosen = jnp.where(jnp.logical_and(named > 0.5, jnp.abs(slot - c) < 0.5), 1.0, 0.0)
            row = jnp.sum(chosen * values, axis=0, keepdims=True)
            for q in range(4):
                pack32[c * 4 + q : c * 4 + q + 1, 0:piece] = row[:, q * piece : (q + 1) * piece]
            total = jnp.sum(chosen * weight, axis=0, keepdims=True)
            pack32[c * 4 : c * 4 + 1, piece : piece + LANES] = jnp.broadcast_to(total, (1, LANES))
        pack[expert] = pack32[...].astype(bf16)

    pl.semaphore_wait(barrier, len(peers))

    sends = []

    def remote(src, dst, peer, chunk, number):
        copy = pltpu.make_async_remote_copy(
            src_ref=src,
            dst_ref=dst,
            send_sem=send_sem.at[chunk, number],
            recv_sem=recv_sem.at[chunk, number],
            device_id=peer,
            device_id_type=MESH,
        )
        copy.start()
        sends.append(copy)
        return copy

    y_copies = []
    for k in (1, 2, 3):
        target = y_peer(k)
        copy = pltpu.make_async_remote_copy(
            src_ref=pack.at[target[0] // 2],
            dst_ref=ybuf.at[y],
            send_sem=ysend_sem.at[k - 1],
            recv_sem=yrecv_sem.at[k - 1],
            device_id=target,
            device_id_type=MESH,
        )
        copy.start()
        sends.append(copy)
        y_copies.append(copy)
    ybuf[y] = pack[y // 2]

    loads[0].wait()

    def split_enc(i):
        r = pl.ds(pl.multiple_of(i * 128, 128), 128)
        enc_w[r, 0:features], enc_w[r, features : 2 * features] = split(enc_stage[r, :])

    each(width // 128, split_enc)

    for copy in y_copies:
        copy.wait_recv()
    for s in range(4):
        came = ybuf[s].astype(f32)
        for c in range(4):
            for q in range(4):
                at = LANES + q * piece
                unit32[s * 4 + c : s * 4 + c + 1, at : at + piece] = came[c * 4 + q : c * 4 + q + 1, 0:piece]
            unit32[s * 4 + c : s * 4 + c + 1, 0:LANES] = came[c * 4 : c * 4 + 1, piece : piece + LANES]
    own_unit = (core * 16 + b * 4 + a) * UNIT
    trows[al(own_unit, UNIT), :] = unit32[...].astype(bf16)

    def block_rows(k):
        return core * HALF + lax.rem(b + k, 4) * BLOCK

    def gather_stages(ref, lane_ranges, base):
        copies = {}

        def go(k, start, size, peer, number):
            part = ref.at[al(start, size), lane_ranges[k]]
            copies[k, number] = remote(part, part, peer, k, base + number)

        def along_a(k):
            for i in (1, 2, 3):
                go(k, own_unit, UNIT, a_peer(i), i - 1)

        def along_b(k):
            for i in (1, 2, 3):
                copies[k, i - 1].wait_recv()
            go(k, block_rows(0), BLOCK, b_peer(1), 3)
            go(k, block_rows(0), BLOCK, b_peer(3), 4)
            go(k, block_rows(0), BLOCK, sibling, 7)

        def onward(k):
            copies[k, 3].wait_recv()
            go(k, block_rows(3), BLOCK // 2, b_peer(1), 5)
            go(k, block_rows(3), BLOCK, sibling, 8)
            copies[k, 4].wait_recv()
            go(k, block_rows(1) + BLOCK // 2, BLOCK // 2, b_peer(3), 6)
            go(k, block_rows(1), BLOCK, sibling, 9)

        def last(k):
            copies[k, 5].wait_recv()
            copies[k, 6].wait_recv()
            go(k, block_rows(2), BLOCK, sibling, 10)

        def arrived(k):
            for number in (7, 8, 9, 10):
                copies[k, number].wait_recv()

        return [along_a, along_b, onward, last, arrived]

    def run(stages, skew):
        tasks = [(s + skew * k, -s, k) for s in range(len(stages)) for k in range(CHUNKS)]
        for _, s, k in sorted(tasks):
            stages[-s](k)

    token_lanes = [
        pl.ds(0, LANES + cols) if k == 0 else pl.ds(LANES + k * cols, cols) for k in range(CHUNKS)
    ]

    def project(k):
        def step(i):
            r = pl.ds(pl.multiple_of(i * 256, 256), 256)
            part = trows[r, LANES + k * cols : LANES + (k + 1) * cols]
            depth = slice(k * cols, (k + 1) * cols)
            gate = dot(part, gate_w[depth, :])
            up = dot(part, up_w[depth, :])
            pre = dot(part, enc_w[depth, :])
            if k > 0:
                gate += acc_gate[r, :]
                up += acc_up[r, :]
                pre += acc_pre[r, :]
            acc_gate[r, :] = gate
            acc_up[r, :] = up
            acc_pre[r, :] = pre

        each(ROWS // 256, step)

    stages = gather_stages(trows, token_lanes, 0)
    for k in range(CHUNKS):
        stages[0](k)

    loads[1].wait()

    def split_dec(i):
        r = pl.ds(pl.multiple_of(i * 16, 16), 16)
        high, low = split(dec_stage[r, :])
        dec_w[r, :] = high
        dec_w[pl.ds(pl.multiple_of(features + i * 16, 16), 16), :] = low
        dec_w[pl.ds(pl.multiple_of(2 * features + i * 16, 16), 16), :] = high

    each(features // 16, split_dec)
    for load in loads[2:]:
        load.wait()
    filled = 3 * features + hidden_width
    dec_w[filled : dec_w.shape[0], :] = jnp.zeros((dec_w.shape[0] - filled, width), bf16)
    left[:, 3 * features + hidden_width - hidden_width % LANES : left.shape[1]] = jnp.zeros(
        (ROWS, left.shape[1] - 3 * features - hidden_width + hidden_width % LANES), bf16
    )
    run(stages[1:] + [project], 1)

    rows_copy = pltpu.make_async_copy(trows.at[:, pl.ds(LANES, width)], rows_out, local_sem.at[5])
    rows_copy.start()

    threshold = jnp.exp(log_threshold[...])

    def activate(i):
        r = pl.ds(pl.multiple_of(i * 64, 64), 64)
        gate = acc_gate[r, :]
        hidden = (gate / (1.0 + jnp.exp(-gate)) * acc_up[r, :]).astype(bf16)
        left[r, 3 * features : 3 * features + hidden_width] = -hidden
        preact = acc_pre[r, 0:features] + acc_pre[r, features : 2 * features] + bias[...]
        shifted = preact - threshold
        soft_gate = 1.0 / (1.0 + jnp.exp(-shifted / sharpness))
        active = preact * soft_gate
        gate_s[r, :] = soft_gate
        shift_s[r, :] = shifted
        high, low = split(active)
        left[r, 0:features] = high
        left[r, features : 2 * features] = high
        left[r, 2 * features : 3 * features] = low
        acc_grad[r, :] = active

    each(ROWS // 64, activate)

    base = 11
    copies = {}

    def reconstruct(k):
        tile = 512

        def mul(start, out):
            def step(n):
                at = pl.ds(pl.multiple_of(k * cols + n * tile, tile), tile)
                out[:, pl.ds(pl.multiple_of(n * tile, tile), tile)] = dot(left[al(start, HALF), :], dec_w[:, at])

            each(cols // tile, step)

        mul((1 - core) * HALF, psib)

        def code(i):
            r = pl.ds(pl.multiple_of(i * 16, 16), 16)
            encode(psib[r, :], sib_out.at[k], r)

        each(HALF // 16, code)
        copies[k, 0] = remote(sib_out.at[k], sib_in.at[k], sibling, k, base)
        mul(core * HALF, pown.at[k])

    def own_rows(k, start):
        return al(lax.rem(b + k, 4) * BLOCK + start, UNIT)

    def code_rows(k, shift, start, count, out, at, extra=None):
        def step(i):
            value = pown[k, own_rows(shift, start + i * UNIT), :]
            if extra is not None:
                value += decode(extra, al(i * UNIT, UNIT))
            encode(value, out, al(at + i * UNIT, UNIT))

        each(count // UNIT, step)

    half = BLOCK // 2

    def sum_cores(k):
        copies[k, 0].wait_recv()

        def step(i):
            r = pl.ds(pl.multiple_of(i * 16, 16), 16)
            pown[k, r, :] += decode(sib_in.at[k], r)

        each(HALF // 16, step)
        code_rows(k, 2, 0, half, b1_out.at[k, 0], 0)
        code_rows(k, 1, half, half, b1_out.at[k, 0], half)
        copies[k, 1] = remote(b1_out.at[k, 0], b1_in.at[k, 0], b_peer(1), k, base + 1)
        code_rows(k, 2, half, half, b1_out.at[k, 1], 0)
        code_rows(k, 3, 0, half, b1_out.at[k, 1], half)
        copies[k, 2] = remote(b1_out.at[k, 1], b1_in.at[k, 1], b_peer(3), k, base + 2)

    def pass_on(k):
        copies[k, 1].wait_recv()
        code_rows(k, 1, 0, half, b2_out.at[k, 0], 0, b1_in.at[k, 0])
        copies[k, 3] = remote(b2_out.at[k, 0], b2_in.at[k, 0], b_peer(1), k, base + 3)
        copies[k, 2].wait_recv()
        code_rows(k, 3, half, half, b2_out.at[k, 1], 0, b1_in.at[k, 1])
        copies[k, 4] = remote(b2_out.at[k, 1], b2_in.at[k, 1], b_peer(3), k, base + 4)

    def sum_b(k):
        copies[k, 3].wait_recv()
        copies[k, 4].wait_recv()

        def step(i):
            r = al(i * UNIT, UNIT)
            far = al(half + i * UNIT, UNIT)
            pown[k, own_rows(0, i * UNIT), :] += decode(b2_in.at[k, 0], r) + decode(b1_in.at[k, 1], far)
            pown[k, own_rows(0, half + i * UNIT), :] += decode(b2_in.at[k, 1], r) + decode(b1_in.at[k, 0], far)

        each(half // UNIT, step)
        for i in (1, 2, 3):
            target = lax.rem(a + i, 4) * UNIT
            encode(pown[k, own_rows(0, target), :], a_out.at[k, i - 1], pl.ds(0, UNIT))
            copies[k, 4 + i] = remote(a_out.at[k, i - 1], a_in.at[k, i - 1], a_peer(i), k, base + 4 + i)

    def sum_a(k):
        r = pl.ds(0, UNIT)
        value = pown[k, own_rows(0, a * UNIT), :]
        for i in (1, 2, 3):
            copies[k, 4 + i].wait_recv()
            value += decode(a_in.at[k, i - 1], r)
        pown[k, own_rows(0, a * UNIT), :] = value
        encode(value, y_out.at[k], r)
        copies[k, 8] = remote(y_out.at[k], y_in.at[k], partner, k, base + 8)

    grad_lanes = [pl.ds(k * cols, cols) for k in range(CHUNKS)]
    grad_stages = gather_stages(rgrad, grad_lanes, 20)

    def sum_y(k):
        copies[k, 8].wait_recv()
        value = pown[k, own_rows(0, a * UNIT), :] + decode(y_in.at[k], pl.ds(0, UNIT))
        weight = trows[al(own_unit, UNIT), 0:LANES].astype(f32)[:, 0:1]
        rgrad[al(own_unit, UNIT), k * cols : (k + 1) * cols] = (2.0 * weight * value).astype(bf16)
        grad_stages[0](k)

    grad_copies = []
    act_part = acc_pre

    def back(k):
        grad_copy = pltpu.make_async_copy(
            rgrad.at[:, pl.ds(k * cols, cols)], grad_out.at[:, pl.ds(k * cols, cols)], local_sem.at[6 + k]
        )
        grad_copy.start()
        grad_copies.append(grad_copy)

        def step(i):
            r = pl.ds(pl.multiple_of(i * 256, 256), 256)
            at = slice(k * cols, (k + 1) * cols)
            part = dot_nt(rgrad[r, at], dec_w[0 : 2 * features, at])
            if k > 0:
                part += act_part[r, :]
            act_part[r, :] = part

        each(ROWS // 256, step)

    def transpose_active(i):
        r = pl.ds(pl.multiple_of(i * 128, 128), 128)
        high, low = split(acc_grad[r, :].T)
        act_high_out[:, r] = high
        act_low_out[:, r] = low

    def start_sums(k):
        reconstruct(k)
        if k == CHUNKS - 1:
            each(ROWS // 128, transpose_active)

    run([start_sums, sum_cores, pass_on, sum_b, sum_a, sum_y] + grad_stages[1:] + [back], 1)

    def finish(i, carry):
        bias_sum, slope_sum = carry
        r = pl.ds(pl.multiple_of(i * 64, 64), 64)
        grad_active = act_part[r, 0:features] + act_part[r, features : 2 * features]
        grad_pre = grad_active * gate_s[r, :]
        pre_high_out[r, :], pre_low_out[r, :] = split(grad_pre)
        hat = jnp.maximum(0.0, 1.0 - jnp.abs(shift_s[r, :]) / kernel_width) / kernel_width
        weight = trows[r, 0:LANES].astype(f32)[:, 0:1]
        slope = (grad_active * threshold + density_weight * weight) * hat
        return (
            bias_sum + jnp.sum(grad_pre, axis=0, keepdims=True),
            slope_sum + jnp.sum(slope, axis=0, keepdims=True),
        )

    zero = jnp.zeros((1, features), f32)
    bias_sum, slope_sum = lax.fori_loop(0, ROWS // 64, finish, (zero, zero))
    bias_out[...] = bias_sum
    threshold_out[...] = -threshold * slope_sum

    rows_copy.wait()
    for copy in grad_copies:
        copy.wait()
    for copy in sends:
        copy.wait_send()


def gradient_kernel(rows, grad, act_high, act_low, pre_high, pre_low, enc_out, dec_out):
    dec_out[...] = dot(act_high[...], grad[...]) + dot(act_low[...], grad[...])
    enc_out[...] = dot_tn(rows[...], pre_high[...]) + dot_tn(rows[...], pre_low[...])


def body(
    tokens,
    expert_ids,
    route_weights,
    gate_proj,
    up_proj,
    down_proj,
    enc_weight,
    enc_bias,
    log_threshold,
    dec_weight,
):
    width = tokens.shape[1]
    hidden = gate_proj.shape[1]
    features = enc_weight.shape[1]
    cols = width // CHUNKS
    depth = 3 * features + (hidden + LANES - 1) // LANES * LANES
    vmem = pl.BlockSpec(memory_space=pltpu.VMEM)
    hbm = pl.BlockSpec(memory_space=pl.ANY)
    shape = jax.ShapeDtypeStruct
    coded = jnp.int16
    message = cols + LANES
    outs = pl.pallas_call(
        forward_kernel,
        name="forward",
        out_shape=(
            shape((ROWS, width), bf16),
            shape((ROWS, width), bf16),
            shape((features, ROWS), bf16),
            shape((features, ROWS), bf16),
            shape((ROWS, features), bf16),
            shape((ROWS, features), bf16),
            shape((1, features), f32),
            shape((1, features), f32),
        ),
        in_specs=[vmem] * 5 + [hbm] * 5,
        out_specs=(hbm, hbm) + (vmem,) * 6,
        scratch_shapes=[
            pltpu.VMEM((width, features), f32),
            pltpu.VMEM((features, width), f32),
            pltpu.VMEM((width, hidden), bf16),
            pltpu.VMEM((width, hidden), bf16),
            pltpu.VMEM((width, 2 * features), bf16),
            pltpu.VMEM((depth, width), bf16),
            pltpu.VMEM((UNIT, width // 4 + LANES), f32),
            pltpu.VMEM((2, UNIT, width // 4 + LANES), bf16),
            pltpu.VMEM((4, UNIT, width // 4 + LANES), bf16),
            pltpu.VMEM((UNIT, width + LANES), f32),
            pltpu.VMEM((ROWS, width + LANES), bf16),
            pltpu.VMEM((ROWS, width), bf16),
            pltpu.VMEM((ROWS, hidden), f32),
            pltpu.VMEM((ROWS, hidden), f32),
            pltpu.VMEM((ROWS, 2 * features), f32),
            pltpu.VMEM((ROWS, depth), bf16),
            pltpu.VMEM((ROWS, features), f32),
            pltpu.VMEM((ROWS, features), f32),
            pltpu.VMEM((ROWS, features), f32),
            pltpu.VMEM((HALF, cols), f32),
            pltpu.VMEM((CHUNKS, HALF, cols), f32),
            pltpu.VMEM((CHUNKS, HALF, message), coded),
            pltpu.VMEM((CHUNKS, HALF, message), coded),
            pltpu.VMEM((CHUNKS, 2, BLOCK, message), coded),
            pltpu.VMEM((CHUNKS, 2, BLOCK, message), coded),
            pltpu.VMEM((CHUNKS, 2, BLOCK // 2, message), coded),
            pltpu.VMEM((CHUNKS, 2, BLOCK // 2, message), coded),
            pltpu.VMEM((CHUNKS, 3, UNIT, message), coded),
            pltpu.VMEM((CHUNKS, 3, UNIT, message), coded),
            pltpu.VMEM((CHUNKS, UNIT, message), coded),
            pltpu.VMEM((CHUNKS, UNIT, message), coded),
            pltpu.SemaphoreType.DMA((CHUNKS, 31)),
            pltpu.SemaphoreType.DMA((CHUNKS, 31)),
            pltpu.SemaphoreType.DMA((3,)),
            pltpu.SemaphoreType.DMA((3,)),
            pltpu.SemaphoreType.DMA((6 + CHUNKS,)),
        ],
        compiler_params=pltpu.CompilerParams(
            collective_id=0, has_side_effects=True, vmem_limit_bytes=60 * 1024 * 1024
        ),
    )(
        tokens,
        expert_ids,
        route_weights,
        enc_bias.reshape(1, -1),
        log_threshold.reshape(1, -1),
        gate_proj,
        up_proj,
        down_proj,
        enc_weight,
        dec_weight,
    )
    rows, grad, act_high, act_low, pre_high, pre_low, grad_bias, grad_threshold = outs
    tile = 512
    whole = lambda i: (0, 0)
    grad_encoder, grad_decoder = pl.pallas_call(
        gradient_kernel,
        name="gradients",
        grid=(width // tile,),
        out_shape=(shape((width, features), f32), shape((features, width), f32)),
        in_specs=[
            pl.BlockSpec((ROWS, tile), lambda i: (0, i)),
            pl.BlockSpec((ROWS, tile), lambda i: (0, i)),
            pl.BlockSpec((features, ROWS), whole),
            pl.BlockSpec((features, ROWS), whole),
            pl.BlockSpec((ROWS, features), whole),
            pl.BlockSpec((ROWS, features), whole),
        ],
        out_specs=(
            pl.BlockSpec((tile, features), lambda i: (i, 0)),
            pl.BlockSpec((features, tile), lambda i: (0, i)),
        ),
        compiler_params=pltpu.CompilerParams(vmem_limit_bytes=32 * 1024 * 1024),
    )(rows, grad, act_high, act_low, pre_high, pre_low)
    return (grad_encoder, grad_decoder, grad_bias.reshape(-1), grad_threshold.reshape(-1))


def solution(mesh):
    in_specs = (
        P(("expert", "feat"), None),
        P(("expert", "feat"), None),
        P(("expert", "feat"), None),
        P(None, ("expert", "feat")),
        P(None, ("expert", "feat")),
        P(("expert", "feat"), None),
        P(None, ("expert", "feat")),
        P(("expert", "feat")),
        P(("expert", "feat")),
        P(("expert", "feat"), None),
    )
    out_specs = (
        P(None, ("expert", "feat")),
        P(("expert", "feat"), None),
        P(("expert", "feat")),
        P(("expert", "feat")),
    )
    return jax.shard_map(body, mesh=mesh, in_specs=in_specs, out_specs=out_specs, check_vma=False)
```

```python
import functools

import jax
import jax.numpy as jnp
from jax import lax
from jax.experimental import pallas as pl
from jax.experimental.pallas import tpu as pltpu
from jax.sharding import PartitionSpec as P

MESH = pl.DeviceIdType.MESH
f32 = jnp.float32
bf16 = jnp.bfloat16

sharpness = 0.1
kernel_width = 0.5
density_weight = 0.01

CHUNKS = 4
GATHER_SPACING = 0.9
SUM_SPACING = 1.0
LANES = 128
UNIT = 16
BLOCK = 4 * UNIT
HALF = 4 * BLOCK
ROWS = 2 * HALF


def dot(left, right):
    return jnp.dot(left, right, preferred_element_type=f32)


def dot_nt(left, right):
    return lax.dot_general(left, right, (((1,), (1,)), ((), ())), preferred_element_type=f32)


def dot_tn(left, right):
    return lax.dot_general(left, right, (((0,), (0,)), ((), ())), preferred_element_type=f32)


def split(value):
    high = value.astype(bf16)
    return high, (value - high.astype(f32)).astype(bf16)


def widest(value, so_far):
    for at in range(0, value.shape[1], LANES):
        so_far = jnp.maximum(so_far, jnp.abs(value[:, at : at + LANES]))
    return so_far


def exponent(so_far):
    largest = jnp.max(so_far, axis=(0, 1), keepdims=True)
    return jnp.broadcast_to(jnp.ceil(jnp.log2(jnp.maximum(largest, 1e-30))), so_far.shape)


def over(tile, width):
    return jnp.concatenate([tile] * (width // LANES), axis=1)


def encode(value, power, out, rows):
    width = value.shape[1]
    out[rows, 0:width] = jnp.round(value * over(jnp.exp2(14.0 - power), width)).astype(jnp.int32).astype(jnp.int16)
    out[rows, width : width + LANES] = power.astype(jnp.int32).astype(jnp.int16)


def decode(ref, rows):
    width = ref.shape[1] - LANES
    scale = jnp.exp2(ref[rows, width : width + LANES].astype(jnp.int32).astype(f32) - 14.0)
    return ref[rows, 0:width].astype(jnp.int32).astype(f32) * over(scale, width)


def each(count, step):
    lax.fori_loop(0, count, lambda i, carry: (step(i), carry)[1], 0)


def al(start, size):
    return pl.ds(pl.multiple_of(start, 16), size)


def forward_kernel(
    tokens,
    ids,
    weights,
    bias,
    log_threshold,
    gate_hbm,
    up_hbm,
    down_hbm,
    enc_hbm,
    dec_hbm,
    rows_out,
    dec_out,
    pre_out,
    bias_out,
    threshold_out,
    enc_stage,
    dec_stage,
    gate_w,
    up_w,
    enc_w,
    dec_w,
    pack32,
    pack,
    ybuf,
    unit32,
    trows,
    rgrad,
    act_s,
    acc_gate,
    acc_up,
    acc_pre,
    left,
    gate_s,
    shift_s,
    acc_grad,
    psib,
    pown,
    sib_out,
    sib_in,
    b1_out,
    b1_in,
    b2_out,
    b2_in,
    a_out,
    a_in,
    y_out,
    y_in,
    send_sem,
    recv_sem,
    ysend_sem,
    yrecv_sem,
    local_sem,
):
    width = tokens.shape[1]
    cols = width // CHUNKS
    hidden_width = gate_w.shape[0]
    features = enc_w.shape[1] // 2
    piece = width // 4

    y = lax.axis_index("expert")
    feat = lax.axis_index("feat")
    core = lax.rem(feat, 2)
    z = lax.rem(feat // 2, 4)
    x = feat // 8
    a = x + core * (z - x)
    b = z + core * (x - z)

    def a_peer(k):
        ax = lax.rem(x + (1 - core) * k, 4)
        az = lax.rem(z + core * k, 4)
        return (y, (ax * 4 + az) * 2 + core)

    def b_peer(k):
        bx = lax.rem(x + core * k, 4)
        bz = lax.rem(z + (1 - core) * k, 4)
        return (y, (bx * 4 + bz) * 2 + core)

    def y_peer(k):
        return (lax.rem(y + k, 4), feat)

    sibling = (y, feat + 1 - 2 * core)
    partner = (y + 1 - 2 * lax.rem(y, 2), feat)

    loads = [
        pltpu.make_async_copy(src, dst, local_sem.at[i])
        for i, (src, dst) in enumerate(
            [
                (enc_hbm, enc_stage),
                (dec_hbm, dec_stage),
                (gate_hbm, gate_w),
                (up_hbm, up_w),
                (down_hbm, dec_w.at[pl.ds(3 * features, hidden_width)]),
            ]
        )
    ]
    for load in loads:
        load.start()

    barrier = pltpu.get_barrier_semaphore()
    peers = [a_peer(k) for k in (1, 2, 3)] + [b_peer(k) for k in (1, 3)] + [y_peer(k) for k in (1, 2, 3)] + [sibling]
    for peer in peers:
        pl.semaphore_signal(barrier, inc=1, device_id=peer, device_id_type=MESH)

    row_id = lax.broadcasted_iota(jnp.int32, (8, 1), 0)
    values = tokens[...].astype(f32)
    route = weights[...].astype(f32)
    diagonal = row_id == lax.broadcasted_iota(jnp.int32, (8, 8), 1)

    def upright(row):
        return jnp.sum(jnp.where(diagonal, jnp.broadcast_to(row, (8, 8)), 0.0), axis=1, keepdims=True)

    for expert in range(2):
        match = ids[...] == expert
        named = upright(jnp.sum(jnp.where(match, 1.0, 0.0), axis=0, keepdims=True))
        weight = upright(jnp.sum(jnp.where(match, route, 0.0), axis=0, keepdims=True))
        slot = jnp.zeros((8, 1), f32)
        for t in range(7):
            slot += jnp.where(row_id > t, named[t : t + 1, :], 0.0)
        pack32[...] = jnp.zeros_like(pack32)
        for c in range(4):
            chosen = jnp.where(jnp.logical_and(named > 0.5, jnp.abs(slot - c) < 0.5), 1.0, 0.0)
            row = jnp.sum(chosen * values, axis=0, keepdims=True)
            for q in range(4):
                pack32[c * 4 + q : c * 4 + q + 1, 0:piece] = row[:, q * piece : (q + 1) * piece]
            total = jnp.sum(chosen * weight, axis=0, keepdims=True)
            pack32[c * 4 : c * 4 + 1, piece : piece + LANES] = jnp.broadcast_to(total, (1, LANES))
        pack[expert] = pack32[...].astype(bf16)

    pl.semaphore_wait(barrier, len(peers))

    sends = []

    def remote(src, dst, peer, chunk, number):
        copy = pltpu.make_async_remote_copy(
            src_ref=src,
            dst_ref=dst,
            send_sem=send_sem.at[chunk, number],
            recv_sem=recv_sem.at[chunk, number],
            device_id=peer,
            device_id_type=MESH,
        )
        copy.start()
        sends.append(copy)
        return copy

    y_copies = []
    for k in (1, 2, 3):
        target = y_peer(k)
        copy = pltpu.make_async_remote_copy(
            src_ref=pack.at[target[0] // 2],
            dst_ref=ybuf.at[y],
            send_sem=ysend_sem.at[k - 1],
            recv_sem=yrecv_sem.at[k - 1],
            device_id=target,
            device_id_type=MESH,
        )
        copy.start()
        sends.append(copy)
        y_copies.append(copy)
    ybuf[y] = pack[y // 2]

    loads[0].wait()

    def split_enc(i):
        r = pl.ds(pl.multiple_of(i * 128, 128), 128)
        enc_w[r, 0:features], enc_w[r, features : 2 * features] = split(enc_stage[r, :])

    each(width // 128, split_enc)

    for copy in y_copies:
        copy.wait_recv()
    for s in range(4):
        came = ybuf[s].astype(f32)
        for c in range(4):
            for q in range(4):
                at = LANES + q * piece
                unit32[s * 4 + c : s * 4 + c + 1, at : at + piece] = came[c * 4 + q : c * 4 + q + 1, 0:piece]
            unit32[s * 4 + c : s * 4 + c + 1, 0:LANES] = came[c * 4 : c * 4 + 1, piece : piece + LANES]
    own_unit = (core * 16 + b * 4 + a) * UNIT
    trows[al(own_unit, UNIT), :] = unit32[...].astype(bf16)

    def block_rows(k):
        return core * HALF + lax.rem(b + k, 4) * BLOCK

    def gather_stages(ref, lane_ranges, base):
        copies = {}

        def go(k, start, size, peer, number):
            part = ref.at[al(start, size), lane_ranges[k]]
            copies[k, number] = remote(part, part, peer, k, base + number)

        def along_a(k):
            for i in (1, 2, 3):
                go(k, own_unit, UNIT, a_peer(i), i - 1)

        def along_b(k):
            for i in (1, 2, 3):
                copies[k, i - 1].wait_recv()
            go(k, block_rows(0), BLOCK, b_peer(1), 3)
            go(k, block_rows(0), BLOCK, b_peer(3), 4)
            go(k, block_rows(0), BLOCK, sibling, 7)

        def onward(k):
            copies[k, 3].wait_recv()
            go(k, block_rows(3), BLOCK // 2, b_peer(1), 5)
            go(k, block_rows(3), BLOCK, sibling, 8)
            copies[k, 4].wait_recv()
            go(k, block_rows(1) + BLOCK // 2, BLOCK // 2, b_peer(3), 6)
            go(k, block_rows(1), BLOCK, sibling, 9)

        def last(k):
            copies[k, 5].wait_recv()
            copies[k, 6].wait_recv()
            go(k, block_rows(2), BLOCK, sibling, 10)

        def arrived(k):
            for number in (7, 8, 9, 10):
                copies[k, number].wait_recv()

        return [along_a, along_b, onward, last, arrived]

    def run(stages, spacing):
        tasks = [(at + spacing * k, -at, k, stage) for at, stage in stages for k in range(CHUNKS)]
        for _, _, k, stage in sorted(tasks, key=lambda task: task[:3]):
            stage(k)

    token_lanes = [
        pl.ds(0, LANES + cols) if k == 0 else pl.ds(LANES + k * cols, cols) for k in range(CHUNKS)
    ]

    def project(k):
        part = trows[:, LANES + k * cols : LANES + (k + 1) * cols]
        depth = slice(k * cols, (k + 1) * cols)
        gate = dot_nt(part, gate_w[:, depth])
        up = dot_nt(part, up_w[:, depth])
        pre = dot(part, enc_w[depth, :])
        if k > 0:
            gate += acc_gate[...]
            up += acc_up[...]
            pre += acc_pre[...]
        acc_gate[...] = gate
        acc_up[...] = up
        acc_pre[...] = pre

    stages = gather_stages(trows, token_lanes, 0)
    for k in range(CHUNKS):
        stages[0](k)

    loads[1].wait()

    def split_dec(i):
        r = pl.ds(pl.multiple_of(i * 16, 16), 16)
        high, low = split(dec_stage[r, :])
        dec_w[r, :] = high
        dec_w[pl.ds(pl.multiple_of(features + i * 16, 16), 16), :] = low
        dec_w[pl.ds(pl.multiple_of(2 * features + i * 16, 16), 16), :] = high

    each(features // 16, split_dec)
    for load in loads[2:]:
        load.wait()
    filled = 3 * features + hidden_width
    dec_w[filled : dec_w.shape[0], :] = jnp.zeros((dec_w.shape[0] - filled, width), bf16)
    left[:, 3 * features + hidden_width - hidden_width % LANES : left.shape[1]] = jnp.zeros(
        (ROWS, left.shape[1] - 3 * features - hidden_width + hidden_width % LANES), bf16
    )
    def finish_rows(k):
        stages[4](k)
        project(k)

    run([(0, stages[1]), (4.0, stages[2]), (7.0, stages[3]), (9.0, finish_rows)], GATHER_SPACING)

    rows_copy = pltpu.make_async_copy(trows.at[:, pl.ds(LANES, width)], rows_out, local_sem.at[5])
    rows_copy.start()

    threshold = jnp.exp(log_threshold[...])

    def activate(i):
        r = pl.ds(pl.multiple_of(i * 64, 64), 64)
        gate = acc_gate[r, :]
        hidden = (gate / (1.0 + jnp.exp(-gate)) * acc_up[r, :]).astype(bf16)
        left[r, 3 * features : 3 * features + hidden_width] = -hidden
        preact = acc_pre[r, 0:features] + acc_pre[r, features : 2 * features] + bias[...]
        shifted = preact - threshold
        soft_gate = 1.0 / (1.0 + jnp.exp(-shifted / sharpness))
        active = preact * soft_gate
        gate_s[r, :] = soft_gate
        shift_s[r, :] = shifted
        high, low = split(active)
        left[r, 0:features] = high
        left[r, features : 2 * features] = high
        left[r, 2 * features : 3 * features] = low
        acc_grad[r, :] = active

    each(ROWS // 64, activate)

    base = 11
    copies = {}

    none = jnp.zeros((UNIT, LANES), f32)

    def multiply(k, start, out):
        tile = 1024

        def step(n):
            at = pl.ds(pl.multiple_of(k * cols + n * tile, tile), tile)
            out[:, pl.ds(pl.multiple_of(n * tile, tile), tile)] = dot(left[al(start, HALF), :], dec_w[:, at])

        each(cols // tile, step)

    def for_sibling(k):
        multiply(k, (1 - core) * HALF, psib)
        power = exponent(
            lax.fori_loop(0, HALF // UNIT, lambda i, m: widest(psib[al(i * UNIT, UNIT), :], m), none)
        )

        def code(i):
            r = al(i * UNIT, UNIT)
            encode(psib[r, :], power, sib_out.at[k], r)

        each(HALF // UNIT, code)
        copies[k, 0] = remote(sib_out.at[k], sib_in.at[k], sibling, k, base)

    def for_own(k):
        multiply(k, core * HALF, pown.at[k])

    def own_rows(shift, start):
        return al(lax.rem(b + shift, 4) * BLOCK + start, UNIT)

    def add(k, rows, count, came, so_far):
        def step(i, m):
            value = pown[k, rows(i), :]
            for ref, at in came:
                value += decode(ref, al(at + i * UNIT, UNIT))
            pown[k, rows(i), :] = value
            return widest(value, m)

        return lax.fori_loop(0, count // UNIT, step, so_far)

    def code_rows(k, shift, start, count, power, out, at):
        def step(i):
            encode(pown[k, own_rows(shift, start + i * UNIT), :], power, out, al(at + i * UNIT, UNIT))

        each(count // UNIT, step)

    half = BLOCK // 2

    def sum_cores(k):
        copies[k, 0].wait_recv()
        power = exponent(add(k, lambda i: al(i * UNIT, UNIT), HALF, [(sib_in.at[k], 0)], none))
        code_rows(k, 2, 0, half, power, b1_out.at[k, 0], 0)
        code_rows(k, 1, half, half, power, b1_out.at[k, 0], half)
        copies[k, 1] = remote(b1_out.at[k, 0], b1_in.at[k, 0], b_peer(1), k, base + 1)
        code_rows(k, 2, half, half, power, b1_out.at[k, 1], 0)
        code_rows(k, 3, 0, half, power, b1_out.at[k, 1], half)
        copies[k, 2] = remote(b1_out.at[k, 1], b1_in.at[k, 1], b_peer(3), k, base + 2)

    def pass_on(k):
        copies[k, 1].wait_recv()
        power = exponent(add(k, lambda i: own_rows(1, i * UNIT), half, [(b1_in.at[k, 0], 0)], none))
        code_rows(k, 1, 0, half, power, b2_out.at[k, 0], 0)
        copies[k, 3] = remote(b2_out.at[k, 0], b2_in.at[k, 0], b_peer(1), k, base + 3)
        copies[k, 2].wait_recv()
        power = exponent(add(k, lambda i: own_rows(3, half + i * UNIT), half, [(b1_in.at[k, 1], 0)], none))
        code_rows(k, 3, half, half, power, b2_out.at[k, 1], 0)
        copies[k, 4] = remote(b2_out.at[k, 1], b2_in.at[k, 1], b_peer(3), k, base + 4)

    def sum_b(k):
        copies[k, 3].wait_recv()
        copies[k, 4].wait_recv()
        largest = add(
            k, lambda i: own_rows(0, i * UNIT), half, [(b2_in.at[k, 0], 0), (b1_in.at[k, 1], half)], none
        )
        largest = add(
            k, lambda i: own_rows(0, half + i * UNIT), half, [(b2_in.at[k, 1], 0), (b1_in.at[k, 0], half)], largest
        )
        power = exponent(largest)
        for i in (1, 2, 3):
            code_rows(k, 0, lax.rem(a + i, 4) * UNIT, UNIT, power, a_out.at[k, i - 1], 0)
            copies[k, 4 + i] = remote(a_out.at[k, i - 1], a_in.at[k, i - 1], a_peer(i), k, base + 4 + i)

    def sum_a(k):
        for i in (1, 2, 3):
            copies[k, 4 + i].wait_recv()
        largest = add(k, lambda i: own_rows(0, a * UNIT), UNIT, [(a_in.at[k, i], 0) for i in range(3)], none)
        code_rows(k, 0, a * UNIT, UNIT, exponent(largest), y_out.at[k], 0)
        copies[k, 8] = remote(y_out.at[k], y_in.at[k], partner, k, base + 8)

    grad_lanes = [pl.ds(k * cols, cols) for k in range(CHUNKS)]
    grad_stages = gather_stages(rgrad, grad_lanes, 20)

    def sum_y(k):
        copies[k, 8].wait_recv()
        value = pown[k, own_rows(0, a * UNIT), :] + decode(y_in.at[k], al(0, UNIT))
        weight = trows[al(own_unit, UNIT), 0:LANES].astype(f32)[:, 0:1]
        rgrad[al(own_unit, UNIT), k * cols : (k + 1) * cols] = (2.0 * weight * value).astype(bf16)
        grad_stages[0](k)

    dec_copies = []
    act_part = acc_pre

    def back(k):
        at = slice(k * cols, (k + 1) * cols)
        part = rgrad[:, at]
        both = dot(act_s[...], part)
        dec_stage[:, at] = both[0:features, :] + both[features : 2 * features, :]
        chunk = pl.ds(k * cols, cols)
        dec_copy = pltpu.make_async_copy(dec_stage.at[:, chunk], dec_out.at[:, chunk], local_sem.at[6 + k])
        dec_copy.start()
        dec_copies.append(dec_copy)
        total = dot_nt(part, dec_w[0 : 2 * features, at])
        if k > 0:
            total += act_part[...]
        act_part[...] = total

    def transpose_active(i):
        r = pl.ds(pl.multiple_of(i * 128, 128), 128)
        act_s[0:features, r], act_s[features : 2 * features, r] = split(acc_grad[r, :].T)

    def last_sum(k):
        if k == CHUNKS - 1:
            each(ROWS // 128, transpose_active)
        pass_on(k)

    run(
        [
            (0, for_sibling),
            (0.7, for_own),
            (3.0, sum_cores),
            (6.7, last_sum),
            (9.7, sum_b),
            (12.7, sum_a),
            (15.7, sum_y),
            (18.7, grad_stages[1]),
            (22.5, grad_stages[2]),
            (25.5, grad_stages[3]),
            (27.5, lambda k: (grad_stages[4](k), back(k))),
        ],
        SUM_SPACING,
    )

    def finish(i, carry):
        bias_sum, slope_sum = carry
        r = pl.ds(pl.multiple_of(i * 64, 64), 64)
        grad_active = act_part[r, 0:features] + act_part[r, features : 2 * features]
        grad_pre = grad_active * gate_s[r, :]
        pre_out[r, 0:features], pre_out[r, features : 2 * features] = split(grad_pre)
        hat = jnp.maximum(0.0, 1.0 - jnp.abs(shift_s[r, :]) / kernel_width) / kernel_width
        weight = trows[r, 0:LANES].astype(f32)[:, 0:1]
        slope = (grad_active * threshold + density_weight * weight) * hat
        return (
            bias_sum + jnp.sum(grad_pre, axis=0, keepdims=True),
            slope_sum + jnp.sum(slope, axis=0, keepdims=True),
        )

    zero = jnp.zeros((1, features), f32)
    bias_sum, slope_sum = lax.fori_loop(0, ROWS // 64, finish, (zero, zero))
    bias_out[...] = bias_sum
    threshold_out[...] = -threshold * slope_sum

    rows_copy.wait()
    for copy in dec_copies:
        copy.wait()
    for copy in sends:
        copy.wait_send()


def gradient_kernel(rows, dec, pre, bias, slope, enc_out, dec_out, bias_out, slope_out):
    features = enc_out.shape[1]
    bias_out[...] = bias[0, :]
    slope_out[...] = slope[0, :]
    dec_out[...] = dec[...]
    both = dot_tn(rows[...], pre[...])
    enc_out[...] = both[:, 0:features] + both[:, features : 2 * features]


def body(
    tokens,
    expert_ids,
    route_weights,
    gate_proj,
    up_proj,
    down_proj,
    enc_weight,
    enc_bias,
    log_threshold,
    dec_weight,
):
    width = tokens.shape[1]
    hidden = gate_proj.shape[1]
    features = enc_weight.shape[1]
    cols = width // CHUNKS
    depth = 3 * features + (hidden + LANES - 1) // LANES * LANES
    vmem = pl.BlockSpec(memory_space=pltpu.VMEM)
    hbm = pl.BlockSpec(memory_space=pl.ANY)
    shape = jax.ShapeDtypeStruct
    coded = jnp.int16
    message = cols + LANES
    outs = pl.pallas_call(
        forward_kernel,
        name="forward",
        out_shape=(
            shape((ROWS, width), bf16),
            shape((features, width), f32),
            shape((ROWS, 2 * features), bf16),
            shape((1, features), f32),
            shape((1, features), f32),
        ),
        in_specs=[vmem] * 5 + [hbm] * 5,
        out_specs=(hbm, hbm) + (vmem,) * 3,
        scratch_shapes=[
            pltpu.VMEM((width, features), f32),
            pltpu.VMEM((features, width), f32),
            pltpu.VMEM((hidden, width), bf16),
            pltpu.VMEM((hidden, width), bf16),
            pltpu.VMEM((width, 2 * features), bf16),
            pltpu.VMEM((depth, width), bf16),
            pltpu.VMEM((UNIT, width // 4 + LANES), f32),
            pltpu.VMEM((2, UNIT, width // 4 + LANES), bf16),
            pltpu.VMEM((4, UNIT, width // 4 + LANES), bf16),
            pltpu.VMEM((UNIT, width + LANES), f32),
            pltpu.VMEM((ROWS, width + LANES), bf16),
            pltpu.VMEM((ROWS, width), bf16),
            pltpu.VMEM((2 * features, ROWS), bf16),
            pltpu.VMEM((ROWS, hidden), f32),
            pltpu.VMEM((ROWS, hidden), f32),
            pltpu.VMEM((ROWS, 2 * features), f32),
            pltpu.VMEM((ROWS, depth), bf16),
            pltpu.VMEM((ROWS, features), f32),
            pltpu.VMEM((ROWS, features), f32),
            pltpu.VMEM((ROWS, features), f32),
            pltpu.VMEM((HALF, cols), f32),
            pltpu.VMEM((CHUNKS, HALF, cols), f32),
            pltpu.VMEM((CHUNKS, HALF, message), coded),
            pltpu.VMEM((CHUNKS, HALF, message), coded),
            pltpu.VMEM((CHUNKS, 2, BLOCK, message), coded),
            pltpu.VMEM((CHUNKS, 2, BLOCK, message), coded),
            pltpu.VMEM((CHUNKS, 2, BLOCK // 2, message), coded),
            pltpu.VMEM((CHUNKS, 2, BLOCK // 2, message), coded),
            pltpu.VMEM((CHUNKS, 3, UNIT, message), coded),
            pltpu.VMEM((CHUNKS, 3, UNIT, message), coded),
            pltpu.VMEM((CHUNKS, UNIT, message), coded),
            pltpu.VMEM((CHUNKS, UNIT, message), coded),
            pltpu.SemaphoreType.DMA((CHUNKS, 31)),
            pltpu.SemaphoreType.DMA((CHUNKS, 31)),
            pltpu.SemaphoreType.DMA((3,)),
            pltpu.SemaphoreType.DMA((3,)),
            pltpu.SemaphoreType.DMA((6 + CHUNKS,)),
        ],
        compiler_params=pltpu.CompilerParams(
            collective_id=0, has_side_effects=True, vmem_limit_bytes=60 * 1024 * 1024
        ),
    )(
        tokens,
        expert_ids.T,
        route_weights.T,
        enc_bias.reshape(1, -1),
        log_threshold.reshape(1, -1),
        gate_proj.T,
        up_proj.T,
        down_proj,
        enc_weight,
        dec_weight,
    )
    rows, grad_decoder, pre, grad_bias, grad_threshold = outs
    tile = 2048
    whole = lambda i: (0, 0)
    return pl.pallas_call(
        gradient_kernel,
        name="gradients",
        grid=(width // tile,),
        out_shape=(
            shape((width, features), f32),
            shape((features, width), f32),
            shape((features,), f32),
            shape((features,), f32),
        ),
        in_specs=[
            pl.BlockSpec((ROWS, tile), lambda i: (0, i)),
            pl.BlockSpec((features, tile), lambda i: (0, i)),
            pl.BlockSpec((ROWS, 2 * features), whole),
            pl.BlockSpec((1, features), whole),
            pl.BlockSpec((1, features), whole),
        ],
        out_specs=(
            pl.BlockSpec((tile, features), lambda i: (i, 0)),
            pl.BlockSpec((features, tile), lambda i: (0, i)),
            pl.BlockSpec((features,), lambda i: (0,)),
            pl.BlockSpec((features,), lambda i: (0,)),
        ),
        compiler_params=pltpu.CompilerParams(vmem_limit_bytes=60 * 1024 * 1024),
    )(rows, grad_decoder, pre, grad_bias, grad_threshold)


def solution(mesh):
    in_specs = (
        P(("expert", "feat"), None),
        P(("expert", "feat"), None),
        P(("expert", "feat"), None),
        P(None, ("expert", "feat")),
        P(None, ("expert", "feat")),
        P(("expert", "feat"), None),
        P(None, ("expert", "feat")),
        P(("expert", "feat")),
        P(("expert", "feat")),
        P(("expert", "feat"), None),
    )
    out_specs = (
        P(None, ("expert", "feat")),
        P(("expert", "feat"), None),
        P(("expert", "feat")),
        P(("expert", "feat")),
    )
    return jax.shard_map(body, mesh=mesh, in_specs=in_specs, out_specs=out_specs, check_vma=False)
```

```python
import functools

import jax
import jax.numpy as jnp
from jax import lax
from jax.experimental import pallas as pl
from jax.experimental.pallas import tpu as pltpu
from jax.sharding import PartitionSpec as P

MESH = pl.DeviceIdType.MESH
f32 = jnp.float32
bf16 = jnp.bfloat16

sharpness = 0.1
kernel_width = 0.5
density_weight = 0.01

CHUNKS = 4
GATHER_SPACING = 0.9
SUM_SPACING = 1.0
LANES = 128
UNIT = 16
BLOCK = 4 * UNIT
HALF = 4 * BLOCK
ROWS = 2 * HALF


def dot(left, right):
    return jnp.dot(left, right, preferred_element_type=f32)


def dot_nt(left, right):
    return lax.dot_general(left, right, (((1,), (1,)), ((), ())), preferred_element_type=f32)


def dot_tn(left, right):
    return lax.dot_general(left, right, (((0,), (0,)), ((), ())), preferred_element_type=f32)


def split(value):
    high = value.astype(bf16)
    return high, (value - high.astype(f32)).astype(bf16)


def widest(value, so_far):
    for at in range(0, value.shape[1], LANES):
        so_far = jnp.maximum(so_far, jnp.abs(value[:, at : at + LANES]))
    return so_far


def exponent(so_far):
    largest = jnp.max(so_far, axis=(0, 1), keepdims=True)
    return jnp.broadcast_to(jnp.ceil(jnp.log2(jnp.maximum(largest, 1e-30))), so_far.shape)


def over(tile, width):
    return jnp.concatenate([tile] * (width // LANES), axis=1)


def encode(value, power, out, rows):
    width = value.shape[1]
    out[rows, 0:width] = jnp.round(value * over(jnp.exp2(14.0 - power), width)).astype(jnp.int32).astype(jnp.int16)
    out[rows, width : width + LANES] = power.astype(jnp.int32).astype(jnp.int16)


def decode(ref, rows):
    width = ref.shape[1] - LANES
    scale = jnp.exp2(ref[rows, width : width + LANES].astype(jnp.int32).astype(f32) - 14.0)
    return ref[rows, 0:width].astype(jnp.int32).astype(f32) * over(scale, width)


def each(count, step):
    lax.fori_loop(0, count, lambda i, carry: (step(i), carry)[1], 0)


def al(start, size):
    return pl.ds(pl.multiple_of(start, 16), size)


def forward_kernel(
    tokens,
    ids,
    weights,
    bias,
    log_threshold,
    gate_hbm,
    up_hbm,
    down_hbm,
    enc_hbm,
    dec_hbm,
    rows_out,
    dec_out,
    pre_out,
    bias_out,
    threshold_out,
    enc_stage,
    dec_stage,
    gate_w,
    up_w,
    enc_w,
    dec_w,
    pack32,
    pack,
    ybuf,
    unit32,
    trows,
    rgrad,
    act_s,
    acc_gate,
    acc_up,
    acc_pre,
    left,
    gate_s,
    shift_s,
    acc_grad,
    psib,
    pown,
    sib_out,
    sib_in,
    b1_out,
    b1_in,
    b2_out,
    b2_in,
    a_out,
    a_in,
    y_out,
    y_in,
    send_sem,
    recv_sem,
    ysend_sem,
    yrecv_sem,
    local_sem,
):
    width = tokens.shape[1]
    cols = width // CHUNKS
    hidden_width = gate_w.shape[0]
    features = enc_w.shape[1] // 2
    piece = width // 4

    y = lax.axis_index("expert")
    feat = lax.axis_index("feat")
    core = lax.rem(feat, 2)
    z = lax.rem(feat // 2, 4)
    x = feat // 8
    a = x + core * (z - x)
    b = z + core * (x - z)

    def a_peer(k):
        ax = lax.rem(x + (1 - core) * k, 4)
        az = lax.rem(z + core * k, 4)
        return (y, (ax * 4 + az) * 2 + core)

    def b_peer(k):
        bx = lax.rem(x + core * k, 4)
        bz = lax.rem(z + (1 - core) * k, 4)
        return (y, (bx * 4 + bz) * 2 + core)

    def y_peer(k):
        return (lax.rem(y + k, 4), feat)

    sibling = (y, feat + 1 - 2 * core)
    partner = (y + 1 - 2 * lax.rem(y, 2), feat)

    loads = [
        pltpu.make_async_copy(src, dst, local_sem.at[i])
        for i, (src, dst) in enumerate(
            [
                (enc_hbm, enc_stage),
                (dec_hbm, dec_stage),
                (gate_hbm, gate_w),
                (up_hbm, up_w),
                (down_hbm, dec_w.at[pl.ds(3 * features, hidden_width)]),
            ]
        )
    ]
    for load in loads:
        load.start()

    barrier = pltpu.get_barrier_semaphore()
    peers = [a_peer(k) for k in (1, 2, 3)] + [b_peer(k) for k in (1, 3)] + [y_peer(k) for k in (1, 2, 3)] + [sibling]
    for peer in peers:
        pl.semaphore_signal(barrier, inc=1, device_id=peer, device_id_type=MESH)

    row_id = lax.broadcasted_iota(jnp.int32, (8, 1), 0)
    values = tokens[...].astype(f32)
    route = weights[...].astype(f32)
    diagonal = row_id == lax.broadcasted_iota(jnp.int32, (8, 8), 1)

    def upright(row):
        return jnp.sum(jnp.where(diagonal, jnp.broadcast_to(row, (8, 8)), 0.0), axis=1, keepdims=True)

    for expert in range(2):
        match = ids[...] == expert
        named = upright(jnp.sum(jnp.where(match, 1.0, 0.0), axis=0, keepdims=True))
        weight = upright(jnp.sum(jnp.where(match, route, 0.0), axis=0, keepdims=True))
        slot = jnp.zeros((8, 1), f32)
        for t in range(7):
            slot += jnp.where(row_id > t, named[t : t + 1, :], 0.0)
        pack32[...] = jnp.zeros_like(pack32)
        for c in range(4):
            chosen = jnp.where(jnp.logical_and(named > 0.5, jnp.abs(slot - c) < 0.5), 1.0, 0.0)
            row = jnp.sum(chosen * values, axis=0, keepdims=True)
            for q in range(4):
                pack32[c * 4 + q : c * 4 + q + 1, 0:piece] = row[:, q * piece : (q + 1) * piece]
            total = jnp.sum(chosen * weight, axis=0, keepdims=True)
            pack32[c * 4 : c * 4 + 1, piece : piece + LANES] = jnp.broadcast_to(total, (1, LANES))
        pack[expert] = pack32[...].astype(bf16)

    pl.semaphore_wait(barrier, len(peers))

    sends = []

    def remote(src, dst, peer, chunk, number):
        copy = pltpu.make_async_remote_copy(
            src_ref=src,
            dst_ref=dst,
            send_sem=send_sem.at[chunk, number],
            recv_sem=recv_sem.at[chunk, number],
            device_id=peer,
            device_id_type=MESH,
        )
        copy.start()
        sends.append(copy)
        return copy

    y_copies = []
    for k in (1, 2, 3):
        target = y_peer(k)
        copy = pltpu.make_async_remote_copy(
            src_ref=pack.at[target[0] // 2],
            dst_ref=ybuf.at[y],
            send_sem=ysend_sem.at[k - 1],
            recv_sem=yrecv_sem.at[k - 1],
            device_id=target,
            device_id_type=MESH,
        )
        copy.start()
        sends.append(copy)
        y_copies.append(copy)
    ybuf[y] = pack[y // 2]

    loads[0].wait()

    def split_enc(i):
        r = pl.ds(pl.multiple_of(i * 128, 128), 128)
        enc_w[r, 0:features], enc_w[r, features : 2 * features] = split(enc_stage[r, :])

    each(width // 128, split_enc)

    for copy in y_copies:
        copy.wait_recv()
    for s in range(4):
        came = ybuf[s].astype(f32)
        for c in range(4):
            for q in range(4):
                at = LANES + q * piece
                unit32[s * 4 + c : s * 4 + c + 1, at : at + piece] = came[c * 4 + q : c * 4 + q + 1, 0:piece]
            unit32[s * 4 + c : s * 4 + c + 1, 0:LANES] = came[c * 4 : c * 4 + 1, piece : piece + LANES]
    own_unit = (core * 16 + b * 4 + a) * UNIT
    trows[al(own_unit, UNIT), :] = unit32[...].astype(bf16)

    def block_rows(k):
        return core * HALF + lax.rem(b + k, 4) * BLOCK

    def gather_stages(ref, lane_ranges, base):
        copies = {}

        def go(k, start, size, peer, number):
            part = ref.at[al(start, size), lane_ranges[k]]
            copies[k, number] = remote(part, part, peer, k, base + number)

        def along_a(k):
            for i in (1, 3, 2):
                go(k, own_unit, UNIT, a_peer(i), i - 1)

        def pass_unit(k, away, number):
            start = block_rows(0) + lax.rem(a + away, 4) * UNIT
            go(k, start, UNIT, b_peer(1), number)
            go(k, start, UNIT, b_peer(3), number + 1)

        def along_b(k):
            if lane_ranges is token_lanes and k >= 2:
                for number in (3, 4, 11, 12, 13, 14, 15, 16):
                    copies[k - 2, number].wait_send()
                    sends[:] = [c for c in sends if c is not copies[k - 2, number]]
            pass_unit(k, 0, 3)
            for away, number in ((3, 11), (1, 13), (2, 15)):
                copies[k, 3 - away].wait_recv()
                pass_unit(k, away, number)
            go(k, block_rows(0), BLOCK, sibling, 7)

        def onward(k):
            for number in (3, 11, 13, 15):
                copies[k, number].wait_recv()
            go(k, block_rows(3), BLOCK // 2, b_peer(1), 5)
            go(k, block_rows(3), BLOCK, sibling, 8)
            for number in (4, 12, 14, 16):
                copies[k, number].wait_recv()
            go(k, block_rows(1) + BLOCK // 2, BLOCK // 2, b_peer(3), 6)
            go(k, block_rows(1), BLOCK, sibling, 9)

        def last(k):
            copies[k, 5].wait_recv()
            copies[k, 6].wait_recv()
            go(k, block_rows(2), BLOCK, sibling, 10)

        def arrived(k):
            for number in (7, 8, 9, 10):
                copies[k, number].wait_recv()

        return [along_a, along_b, onward, last, arrived]

    def run(stages, spacing):
        tasks = [(at + spacing * k, -at, k, stage) for at, stage in stages for k in range(CHUNKS)]
        for _, _, k, stage in sorted(tasks, key=lambda task: task[:3]):
            stage(k)

    token_lanes = [
        pl.ds(0, LANES + cols) if k == 0 else pl.ds(LANES + k * cols, cols) for k in range(CHUNKS)
    ]

    def project(k):
        part = trows[:, LANES + k * cols : LANES + (k + 1) * cols]
        depth = slice(k * cols, (k + 1) * cols)
        gate = dot_nt(part, gate_w[:, depth])
        up = dot_nt(part, up_w[:, depth])
        pre = dot(part, enc_w[depth, :])
        if k > 0:
            gate += acc_gate[...]
            up += acc_up[...]
            pre += acc_pre[...]
        acc_gate[...] = gate
        acc_up[...] = up
        acc_pre[...] = pre

    stages = gather_stages(trows, token_lanes, 0)
    for k in range(CHUNKS):
        stages[0](k)

    loads[1].wait()

    def split_dec(i):
        r = pl.ds(pl.multiple_of(i * 16, 16), 16)
        high, low = split(dec_stage[r, :])
        dec_w[r, :] = high
        dec_w[pl.ds(pl.multiple_of(features + i * 16, 16), 16), :] = low
        dec_w[pl.ds(pl.multiple_of(2 * features + i * 16, 16), 16), :] = high

    each(features // 16, split_dec)
    for load in loads[2:]:
        load.wait()
    filled = 3 * features + hidden_width
    dec_w[filled : dec_w.shape[0], :] = jnp.zeros((dec_w.shape[0] - filled, width), bf16)
    left[:, 3 * features + hidden_width - hidden_width % LANES : left.shape[1]] = jnp.zeros(
        (ROWS, left.shape[1] - 3 * features - hidden_width + hidden_width % LANES), bf16
    )
    def finish_rows(k):
        stages[4](k)
        project(k)

    run([(0, stages[1]), (4.0, stages[2]), (7.0, stages[3]), (9.0, finish_rows)], GATHER_SPACING)

    rows_copy = pltpu.make_async_copy(trows.at[:, pl.ds(LANES, width)], rows_out, local_sem.at[5])
    rows_copy.start()

    threshold = jnp.exp(log_threshold[...])

    def activate(i):
        r = pl.ds(pl.multiple_of(i * 64, 64), 64)
        gate = acc_gate[r, :]
        hidden = (gate / (1.0 + jnp.exp(-gate)) * acc_up[r, :]).astype(bf16)
        left[r, 3 * features : 3 * features + hidden_width] = -hidden
        preact = acc_pre[r, 0:features] + acc_pre[r, features : 2 * features] + bias[...]
        shifted = preact - threshold
        soft_gate = 1.0 / (1.0 + jnp.exp(-shifted / sharpness))
        active = preact * soft_gate
        gate_s[r, :] = soft_gate
        shift_s[r, :] = shifted
        high, low = split(active)
        left[r, 0:features] = high
        left[r, features : 2 * features] = high
        left[r, 2 * features : 3 * features] = low
        acc_grad[r, :] = active

    each(ROWS // 64, activate)

    base = 17
    copies = {}

    none = jnp.zeros((UNIT, LANES), f32)

    def multiply(k, start, out):
        tile = 1024

        def step(n):
            at = pl.ds(pl.multiple_of(k * cols + n * tile, tile), tile)
            out[:, pl.ds(pl.multiple_of(n * tile, tile), tile)] = dot(left[al(start, HALF), :], dec_w[:, at])

        each(cols // tile, step)

    def for_sibling(k):
        multiply(k, (1 - core) * HALF, psib)
        power = exponent(
            lax.fori_loop(0, HALF // UNIT, lambda i, m: widest(psib[al(i * UNIT, UNIT), :], m), none)
        )

        def code(i):
            r = al(i * UNIT, UNIT)
            encode(psib[r, :], power, sib_out.at[k], r)

        each(HALF // UNIT, code)
        copies[k, 0] = remote(sib_out.at[k], sib_in.at[k], sibling, k, base)

    def for_own(k):
        multiply(k, core * HALF, pown.at[k])

    def own_rows(shift, start):
        return al(lax.rem(b + shift, 4) * BLOCK + start, UNIT)

    def add(k, rows, count, came, so_far):
        def step(i, m):
            value = pown[k, rows(i), :]
            for ref, at in came:
                value += decode(ref, al(at + i * UNIT, UNIT))
            pown[k, rows(i), :] = value
            return widest(value, m)

        return lax.fori_loop(0, count // UNIT, step, so_far)

    def code_rows(k, shift, start, count, power, out, at):
        def step(i):
            encode(pown[k, own_rows(shift, start + i * UNIT), :], power, out, al(at + i * UNIT, UNIT))

        each(count // UNIT, step)

    half = BLOCK // 2

    def sum_cores(k):
        copies[k, 0].wait_recv()
        power = exponent(add(k, lambda i: al(i * UNIT, UNIT), HALF, [(sib_in.at[k], 0)], none))
        code_rows(k, 2, 0, half, power, b1_out.at[k, 0], 0)
        code_rows(k, 1, half, half, power, b1_out.at[k, 0], half)
        copies[k, 1] = remote(b1_out.at[k, 0], b1_in.at[k, 0], b_peer(1), k, base + 1)
        code_rows(k, 2, half, half, power, b1_out.at[k, 1], 0)
        code_rows(k, 3, 0, half, power, b1_out.at[k, 1], half)
        copies[k, 2] = remote(b1_out.at[k, 1], b1_in.at[k, 1], b_peer(3), k, base + 2)

    def pass_on(k):
        copies[k, 1].wait_recv()
        power = exponent(add(k, lambda i: own_rows(1, i * UNIT), half, [(b1_in.at[k, 0], 0)], none))
        code_rows(k, 1, 0, half, power, b2_out.at[k, 0], 0)
        copies[k, 3] = remote(b2_out.at[k, 0], b2_in.at[k, 0], b_peer(1), k, base + 3)
        copies[k, 2].wait_recv()
        power = exponent(add(k, lambda i: own_rows(3, half + i * UNIT), half, [(b1_in.at[k, 1], 0)], none))
        code_rows(k, 3, half, half, power, b2_out.at[k, 1], 0)
        copies[k, 4] = remote(b2_out.at[k, 1], b2_in.at[k, 1], b_peer(3), k, base + 4)

    def sum_b(k):
        copies[k, 3].wait_recv()
        copies[k, 4].wait_recv()
        largest = add(
            k, lambda i: own_rows(0, i * UNIT), half, [(b2_in.at[k, 0], 0), (b1_in.at[k, 1], half)], none
        )
        largest = add(
            k, lambda i: own_rows(0, half + i * UNIT), half, [(b2_in.at[k, 1], 0), (b1_in.at[k, 0], half)], largest
        )
        power = exponent(largest)
        for i in (1, 2, 3):
            code_rows(k, 0, lax.rem(a + i, 4) * UNIT, UNIT, power, a_out.at[k, i - 1], 0)
            copies[k, 4 + i] = remote(a_out.at[k, i - 1], a_in.at[k, i - 1], a_peer(i), k, base + 4 + i)

    def sum_a(k):
        for i in (1, 2, 3):
            copies[k, 4 + i].wait_recv()
        largest = add(k, lambda i: own_rows(0, a * UNIT), UNIT, [(a_in.at[k, i], 0) for i in range(3)], none)
        code_rows(k, 0, a * UNIT, UNIT, exponent(largest), y_out.at[k], 0)
        copies[k, 8] = remote(y_out.at[k], y_in.at[k], partner, k, base + 8)

    grad_lanes = [pl.ds(k * cols, cols) for k in range(CHUNKS)]
    grad_stages = gather_stages(rgrad, grad_lanes, 26)

    def sum_y(k):
        copies[k, 8].wait_recv()
        value = pown[k, own_rows(0, a * UNIT), :] + decode(y_in.at[k], al(0, UNIT))
        weight = trows[al(own_unit, UNIT), 0:LANES].astype(f32)[:, 0:1]
        rgrad[al(own_unit, UNIT), k * cols : (k + 1) * cols] = (2.0 * weight * value).astype(bf16)
        grad_stages[0](k)

    dec_copies = []
    act_part = acc_pre

    def back(k):
        at = slice(k * cols, (k + 1) * cols)
        part = rgrad[:, at]
        both = dot(act_s[...], part)
        dec_stage[:, at] = both[0:features, :] + both[features : 2 * features, :]
        chunk = pl.ds(k * cols, cols)
        dec_copy = pltpu.make_async_copy(dec_stage.at[:, chunk], dec_out.at[:, chunk], local_sem.at[6 + k])
        dec_copy.start()
        dec_copies.append(dec_copy)
        total = dot_nt(part, dec_w[0 : 2 * features, at])
        if k > 0:
            total += act_part[...]
        act_part[...] = total

    def transpose_active(i):
        r = pl.ds(pl.multiple_of(i * 128, 128), 128)
        act_s[0:features, r], act_s[features : 2 * features, r] = split(acc_grad[r, :].T)

    def last_sum(k):
        if k == CHUNKS - 1:
            each(ROWS // 128, transpose_active)
        pass_on(k)

    run(
        [
            (0, for_sibling),
            (0.7, for_own),
            (3.0, sum_cores),
            (6.7, last_sum),
            (9.7, sum_b),
            (12.7, sum_a),
            (15.7, sum_y),
            (18.7, grad_stages[1]),
            (22.5, grad_stages[2]),
            (25.5, grad_stages[3]),
            (27.5, lambda k: (grad_stages[4](k), back(k))),
        ],
        SUM_SPACING,
    )

    def finish(i, carry):
        bias_sum, slope_sum = carry
        r = pl.ds(pl.multiple_of(i * 64, 64), 64)
        grad_active = act_part[r, 0:features] + act_part[r, features : 2 * features]
        grad_pre = grad_active * gate_s[r, :]
        pre_out[r, 0:features], pre_out[r, features : 2 * features] = split(grad_pre)
        hat = jnp.maximum(0.0, 1.0 - jnp.abs(shift_s[r, :]) / kernel_width) / kernel_width
        weight = trows[r, 0:LANES].astype(f32)[:, 0:1]
        slope = (grad_active * threshold + density_weight * weight) * hat
        return (
            bias_sum + jnp.sum(grad_pre, axis=0, keepdims=True),
            slope_sum + jnp.sum(slope, axis=0, keepdims=True),
        )

    zero = jnp.zeros((1, features), f32)
    bias_sum, slope_sum = lax.fori_loop(0, ROWS // 64, finish, (zero, zero))
    bias_out[...] = bias_sum
    threshold_out[...] = -threshold * slope_sum

    rows_copy.wait()
    for copy in dec_copies:
        copy.wait()
    for copy in sends:
        copy.wait_send()


def gradient_kernel(rows, dec, pre, bias, slope, enc_out, dec_out, bias_out, slope_out):
    features = enc_out.shape[1]
    bias_out[...] = bias[0, :]
    slope_out[...] = slope[0, :]
    dec_out[...] = dec[...]
    both = dot_tn(rows[...], pre[...])
    enc_out[...] = both[:, 0:features] + both[:, features : 2 * features]


def body(
    tokens,
    expert_ids,
    route_weights,
    gate_proj,
    up_proj,
    down_proj,
    enc_weight,
    enc_bias,
    log_threshold,
    dec_weight,
):
    width = tokens.shape[1]
    hidden = gate_proj.shape[1]
    features = enc_weight.shape[1]
    cols = width // CHUNKS
    depth = 3 * features + (hidden + LANES - 1) // LANES * LANES
    vmem = pl.BlockSpec(memory_space=pltpu.VMEM)
    hbm = pl.BlockSpec(memory_space=pl.ANY)
    shape = jax.ShapeDtypeStruct
    coded = jnp.int16
    message = cols + LANES
    outs = pl.pallas_call(
        forward_kernel,
        name="forward",
        out_shape=(
            shape((ROWS, width), bf16),
            shape((features, width), f32),
            shape((ROWS, 2 * features), bf16),
            shape((1, features), f32),
            shape((1, features), f32),
        ),
        in_specs=[vmem] * 5 + [hbm] * 5,
        out_specs=(hbm, hbm) + (vmem,) * 3,
        scratch_shapes=[
            pltpu.VMEM((width, features), f32),
            pltpu.VMEM((features, width), f32),
            pltpu.VMEM((hidden, width), bf16),
            pltpu.VMEM((hidden, width), bf16),
            pltpu.VMEM((width, 2 * features), bf16),
            pltpu.VMEM((depth, width), bf16),
            pltpu.VMEM((UNIT, width // 4 + LANES), f32),
            pltpu.VMEM((2, UNIT, width // 4 + LANES), bf16),
            pltpu.VMEM((4, UNIT, width // 4 + LANES), bf16),
            pltpu.VMEM((UNIT, width + LANES), f32),
            pltpu.VMEM((ROWS, width + LANES), bf16),
            pltpu.VMEM((ROWS, width), bf16),
            pltpu.VMEM((2 * features, ROWS), bf16),
            pltpu.VMEM((ROWS, hidden), f32),
            pltpu.VMEM((ROWS, hidden), f32),
            pltpu.VMEM((ROWS, 2 * features), f32),
            pltpu.VMEM((ROWS, depth), bf16),
            pltpu.VMEM((ROWS, features), f32),
            pltpu.VMEM((ROWS, features), f32),
            pltpu.VMEM((ROWS, features), f32),
            pltpu.VMEM((HALF, cols), f32),
            pltpu.VMEM((CHUNKS, HALF, cols), f32),
            pltpu.VMEM((CHUNKS, HALF, message), coded),
            pltpu.VMEM((CHUNKS, HALF, message), coded),
            pltpu.VMEM((CHUNKS, 2, BLOCK, message), coded),
            pltpu.VMEM((CHUNKS, 2, BLOCK, message), coded),
            pltpu.VMEM((CHUNKS, 2, BLOCK // 2, message), coded),
            pltpu.VMEM((CHUNKS, 2, BLOCK // 2, message), coded),
            pltpu.VMEM((CHUNKS, 3, UNIT, message), coded),
            pltpu.VMEM((CHUNKS, 3, UNIT, message), coded),
            pltpu.VMEM((CHUNKS, UNIT, message), coded),
            pltpu.VMEM((CHUNKS, UNIT, message), coded),
            pltpu.SemaphoreType.DMA((CHUNKS, 43)),
            pltpu.SemaphoreType.DMA((CHUNKS, 43)),
            pltpu.SemaphoreType.DMA((3,)),
            pltpu.SemaphoreType.DMA((3,)),
            pltpu.SemaphoreType.DMA((6 + CHUNKS,)),
        ],
        compiler_params=pltpu.CompilerParams(
            collective_id=0, has_side_effects=True, vmem_limit_bytes=60 * 1024 * 1024
        ),
    )(
        tokens,
        expert_ids.T,
        route_weights.T,
        enc_bias.reshape(1, -1),
        log_threshold.reshape(1, -1),
        gate_proj.T,
        up_proj.T,
        down_proj,
        enc_weight,
        dec_weight,
    )
    rows, grad_decoder, pre, grad_bias, grad_threshold = outs
    tile = 2048
    whole = lambda i: (0, 0)
    return pl.pallas_call(
        gradient_kernel,
        name="gradients",
        grid=(width // tile,),
        out_shape=(
            shape((width, features), f32),
            shape((features, width), f32),
            shape((features,), f32),
            shape((features,), f32),
        ),
        in_specs=[
            pl.BlockSpec((ROWS, tile), lambda i: (0, i)),
            pl.BlockSpec((features, tile), lambda i: (0, i)),
            pl.BlockSpec((ROWS, 2 * features), whole),
            pl.BlockSpec((1, features), whole),
            pl.BlockSpec((1, features), whole),
        ],
        out_specs=(
            pl.BlockSpec((tile, features), lambda i: (i, 0)),
            pl.BlockSpec((features, tile), lambda i: (0, i)),
            pl.BlockSpec((features,), lambda i: (0,)),
            pl.BlockSpec((features,), lambda i: (0,)),
        ),
        compiler_params=pltpu.CompilerParams(vmem_limit_bytes=60 * 1024 * 1024),
    )(rows, grad_decoder, pre, grad_bias, grad_threshold)


def solution(mesh):
    in_specs = (
        P(("expert", "feat"), None),
        P(("expert", "feat"), None),
        P(("expert", "feat"), None),
        P(None, ("expert", "feat")),
        P(None, ("expert", "feat")),
        P(("expert", "feat"), None),
        P(None, ("expert", "feat")),
        P(("expert", "feat")),
        P(("expert", "feat")),
        P(("expert", "feat"), None),
    )
    out_specs = (
        P(None, ("expert", "feat")),
        P(("expert", "feat"), None),
        P(("expert", "feat")),
        P(("expert", "feat")),
    )
    return jax.shard_map(body, mesh=mesh, in_specs=in_specs, out_specs=out_specs, check_vma=False)
```
